256 devices in a mesh: section: 16 (over y, x), tensor: 16 (over z, core).
Axes of the slice: x: 4, y: 4, z: 8, core: 2. Of those that a mesh axis runs over, the one named last changes fastest.
Arguments:
- cot_in: bfloat16 [4096, 2304], P(('section', 'tensor')), may hold values from -6 to 6
- saved_inputs: bfloat16 [3, 4096, 2304], P(None, ('section', 'tensor')), may hold values from -6 to 6
- queries: bfloat16 [3, 4096, 4096], P(None, 'section', 'tensor'), may hold values from -120 to 120
- keys: bfloat16 [3, 4096, 2048], P(None, 'section', 'tensor'), may hold values from -6 to 6
- values: bfloat16 [3, 4096, 2048], P(None, 'section', 'tensor'), may hold values from -6 to 6
- docs: int32 [3, 16, 256], P(None, 'section'), may hold values from 0 to 7, never falling along the last dimension, each value on 1 to 128 neighbouring positions
- plan: int32 [3, 16], P(None, 'section'), may hold values from 0 to 1
- w_value: bfloat16 [2, 16, 2304, 2048], P(None, 'section', None, 'tensor'), may hold values from -0.125 to 0.125
- w_out: bfloat16 [2, 16, 4096, 2304], P(None, 'section', 'tensor'), may hold values from -0.09375 to 0.09375
- norm_gain: bfloat16 [2, 16, 2304], P(None, 'section'), may hold values from 0.099609375 to 1.8984375
Outputs:
- cot_out: bfloat16 [4096, 2304], P(('section', 'tensor'))
- grad_queries: bfloat16 [3, 4096, 4096], P(None, 'section', 'tensor')
- grad_keys: bfloat16 [3, 4096, 2048], P(None, 'section', 'tensor')
The draws below stay inside these ranges and needn't reach their ends.
Inputs may be any that keep to these rules, and one draw needn't show every extreme that they name: `docs`: document ids never fall along a sequence.
All inputs are finite; a program needn't handle non-finite values.
Results may differ from the reference program's by a relative error of at most 0.035.
Values may be sent and summed in bfloat16 or wider, within the bound.
No kernel may reach another device: no remote copies, remote signals or barrier semaphores. Data moves between devices by JAX's collectives and lax.ppermute only.
A program may use at most 64 MiB of HBM per device.

```python
import math
import jax
import jax.numpy as jnp
import numpy as np
from jax import lax

D = 2304
HD = 128
QHEADS = 32
KVHEADS = 16
SEQ = 256
TICKS = 3
ROUNDS = 2
QW = 4096
KW = 2048
ROWS = 4096
N_SECTION = 16
N_TENSOR = 16


def shared_keys(key):
    return jnp.clip(jax.random.normal(key, (TICKS, N_SECTION * SEQ, KVHEADS * HD), jnp.float32), -6.0, 6.0)


def draw_keys(key, part):
    return shared_keys(key).astype(jnp.bfloat16)


def draw_queries(key, part):
    key = jax.random.fold_in(key, 5)
    fresh = jax.random.normal(key, (TICKS, N_SECTION * SEQ, QHEADS * HD), jnp.float32)
    return jnp.clip(fresh, -120.0, 120.0).astype(jnp.bfloat16)


def plant(values, own_key, least, high):
    extent = values.shape
    spot = [jax.random.randint(jax.random.fold_in(own_key, axis), (), 0, extent[axis]) for axis in range(len(extent))]
    values = values.at[tuple(spot)].set(least)
    longest = extent.index(max(extent))
    spot[longest] = (spot[longest] + 1) % extent[longest]
    return values.at[tuple(spot)].set(high)


def levels(own_key, shape, shards, smallest, largest):
    factor_of, own = 1.0, jax.random.fold_in(own_key, 6)
    for axis_at, blocks in shards:
        draws = jnp.exp(jax.random.uniform(jax.random.fold_in(own, axis_at), (blocks,), jnp.float32, smallest / len(shards), largest / len(shards)))
        factor_of = factor_of * jnp.repeat(draws, shape[axis_at] // blocks).reshape([-1 if axis == axis_at else 1 for axis in range(len(shape))])
    return factor_of


def profile(count, total, most, slope):
    weights = [(1 << 20) // math.isqrt(rank ** slope) + 1 for rank in range(2, count + 1)]
    surplus, given = total - most - (count - 1), [1] * (count - 1)
    while surplus > 0:
        free = [i for i in range(count - 1) if given[i] < most]
        whole, budget = sum([weights[i] for i in free]), surplus
        for i in free:
            extra = min(most - given[i], max(1, budget * weights[i] // whole), surplus)
            given[i] = given[i] + extra
            surplus = surplus - extra
    return np.array([most] + given)


def uneven_parts(key, amount, total, bound, skew):
    if amount == 2:
        one = jax.random.randint(key, (), max(1, total - bound), min(bound, total - 1) + 1)
        return jnp.stack([one, total - one])
    tallies = jnp.asarray(profile(amount, total, bound, skew), jnp.int32)
    twos = (amount - 1) // 2
    source_of, sink = tallies[1:1 + 2 * twos:2], tallies[2:2 + 2 * twos:2]
    margin = jnp.minimum(source_of - 1, bound - sink)
    moved = jax.random.randint(jax.random.fold_in(key, 1), (twos,), 0, 1 << 20) % (margin + 1)
    tallies = tallies.at[1:1 + 2 * twos:2].set(source_of - moved).at[2:2 + 2 * twos:2].set(sink + moved)
    return tallies[jax.random.permutation(jax.random.fold_in(key, 2), amount)]


def gaussian(stream_key, dims, scale, limit, shards=(), kind=jnp.bfloat16):
    values = jax.random.normal(stream_key, dims, jnp.float32) * scale
    if len(shards) > 0:
        values = levels(stream_key, dims, shards, -0.22, 0.18) * values
    return jnp.clip(values, min=-limit, max=limit).astype(kind)


def setup_inputs(seed: int = 0) -> dict:
    arg_keys = jax.random.split(jax.random.key(seed), 11)
    return {
        "cot_in": gaussian(arg_keys[0], (ROWS, D), 1.0, 6.0, ((0, 256),)),
        "saved_inputs": gaussian(arg_keys[1], (TICKS, ROWS, D), 1.0, 6.0, ((1, 256),)),
        "queries": draw_queries(jax.random.fold_in(arg_keys[10], 71), 0),
        "keys": draw_keys(jax.random.fold_in(arg_keys[10], 71), 0),
        "values": gaussian(arg_keys[4], (TICKS, ROWS, KW), 1.0, 6.0, ((1, 16), (2, 16))),
        "docs": jax.vmap(lambda own: jnp.searchsorted(jnp.cumsum(uneven_parts(own, 8, SEQ, SEQ // 2, 1)), jnp.arange(SEQ), side="right"))(jax.random.split(arg_keys[5], TICKS * N_SECTION)).reshape((TICKS, N_SECTION, SEQ)).astype(jnp.int32),
        "plan": plant(jax.random.randint(arg_keys[6], (TICKS, N_SECTION), 0, ROUNDS), jax.random.fold_in(arg_keys[6], 1), 0, ROUNDS - 1).astype(jnp.int32),
        "w_value": gaussian(arg_keys[7], (ROUNDS, N_SECTION, D, KW), D ** -0.5, 0.125, ((1, 16), (3, 16))),
        "w_out": gaussian(arg_keys[8], (ROUNDS, N_SECTION, QW, D), QW ** -0.5, 0.09375, ((1, 16), (2, 16))),
        "norm_gain": jnp.clip(1.0 + 0.18 * jax.random.normal(arg_keys[9], (ROUNDS, N_SECTION, D), jnp.float32), 0.099609375, 1.8984375).astype(jnp.bfloat16),
    }


SCALE = 144.0 ** (-0.5)
EPS = 1e-06
NEGATIVE = -1e+30

def attention_grads(grad_out, queries, keys, values, docs):
    length = queries.shape[0]
    kv_heads = keys.shape[1] // HD
    group_size = queries.shape[1] // keys.shape[1]
    query_heads = queries.astype(jnp.float32).reshape(length, kv_heads, group_size, HD)
    key_heads = keys.astype(jnp.float32).reshape(length, kv_heads, HD)
    value_heads = values.astype(jnp.float32).reshape(length, kv_heads, HD)
    grad_heads = grad_out.astype(jnp.float32).reshape(length, kv_heads, group_size, HD)
    position = jnp.arange(length, dtype=jnp.int32)
    allowed = (position[:, None] >= position[None, :]) & (docs[:, None] == docs[None, :])
    scores = jnp.einsum('qcgd,kcd->cgqk', query_heads, key_heads) * SCALE
    scores = jnp.where(allowed, scores, NEGATIVE)
    row_max = lax.optimization_barrier(jnp.max(scores, axis=-1, keepdims=True))
    expsum = jnp.exp(scores - row_max)
    chance = expsum / lax.optimization_barrier(jnp.sum(expsum, axis=-1, keepdims=True))
    chance_low = chance.astype(jnp.bfloat16).astype(jnp.float32)
    attended = jnp.einsum('cgqk,kcd->cgqd', chance_low, value_heads)
    row_dot = lax.optimization_barrier(jnp.sum(jnp.transpose(grad_heads, (1, 2, 0, 3)) * attended, axis=-1))
    grad_chance = jnp.einsum('qcgd,kcd->cgqk', grad_heads, value_heads)
    grad_scores = (chance * (grad_chance - row_dot[..., None])).astype(jnp.bfloat16).astype(jnp.float32)
    grad_query = (jnp.einsum('cgqk,kcd->qcgd', grad_scores, key_heads) * SCALE).astype(jnp.bfloat16)
    grad_key = (jnp.einsum('cgqk,qcgd->kcd', grad_scores, query_heads) * SCALE).astype(jnp.bfloat16)
    grad_value = jnp.einsum('cgqk,qcgd->kcd', chance_low, grad_heads).astype(jnp.bfloat16)
    return (grad_query.reshape(length, -1), grad_key.reshape(length, -1), grad_value.reshape(length, -1))

def norm_back(cotangent, inputs, gain_row, summed):
    inputs_wide = inputs.astype(jnp.float32)
    inverse = lax.rsqrt(lax.optimization_barrier(jnp.mean(inputs_wide * inputs_wide, axis=-1, keepdims=True)) + EPS)
    scaled = summed * gain_row.astype(jnp.float32)
    inner_mean = lax.optimization_barrier(jnp.mean(scaled * inputs_wide, axis=-1, keepdims=True))
    updated = cotangent.astype(jnp.float32) + inverse * scaled - inputs_wide * inverse * inverse * inverse * inner_mean
    return updated.astype(jnp.bfloat16)

def by_group(array):
    return jnp.moveaxis(array.reshape(array.shape[0], N_TENSOR, -1), 1, 0)

def from_group(array):
    return jnp.moveaxis(array, 0, 1).reshape(array.shape[1], -1)

def phase_backward(cotangent, inputs, queries, keys, values, docs, gain_row, value_weight, out_weight):
    grad_out = jnp.dot(cotangent, out_weight.T, preferred_element_type=jnp.float32).astype(jnp.bfloat16)

    def per_group(group_items):
        group_out, group_query, group_key, group_value, group_weight = group_items
        grad_query, grad_key, grad_value = attention_grads(group_out, group_query, group_key, group_value, docs)
        partial_sum = jnp.dot(grad_value, group_weight.T, preferred_element_type=jnp.float32).astype(jnp.bfloat16)
        return (grad_query, grad_key, partial_sum)
    weight_groups = jnp.moveaxis(value_weight.reshape(value_weight.shape[0], N_TENSOR, -1), 1, 0)
    grad_query, grad_key, partials = lax.map(per_group, (by_group(grad_out), by_group(queries), by_group(keys), by_group(values), weight_groups))
    summed = lax.optimization_barrier(jnp.sum(partials.astype(jnp.float32), axis=0))
    updated = norm_back(cotangent, inputs, gain_row, summed)
    return (updated, from_group(grad_query), from_group(grad_key))

def reference(cot_in, saved_inputs, queries, keys, values, docs, plan, w_value, w_out, norm_gain):
    cotangent = cot_in.reshape(N_SECTION, SEQ, D)
    query_list = []
    key_list = []
    for step_index in range(TICKS):

        def one_phase(phase_items):
            phase_index, phase_cot, phase_inputs, phase_query, phase_key, phase_value, phase_docs = phase_items
            chosen = plan[step_index, phase_index]
            return phase_backward(phase_cot, phase_inputs, phase_query, phase_key, phase_value, phase_docs, norm_gain[chosen, phase_index], w_value[chosen, phase_index], w_out[chosen, phase_index])
        phase_items = (jnp.arange(N_SECTION, dtype=jnp.int32), cotangent, saved_inputs[step_index].reshape(N_SECTION, SEQ, D), queries[step_index].reshape(N_SECTION, SEQ, QW), keys[step_index].reshape(N_SECTION, SEQ, KW), values[step_index].reshape(N_SECTION, SEQ, KW), docs[step_index])
        updated, grad_query, grad_key = lax.map(one_phase, phase_items)
        cotangent = jnp.roll(updated, -1, axis=0)
        query_list.append(grad_query.reshape(ROWS, QW))
        key_list.append(grad_key.reshape(ROWS, KW))
    return (cotangent.reshape(ROWS, D), jnp.stack(query_list), jnp.stack(key_list))
```

```python
import jax
import jax.numpy as jnp
from jax import lax
from jax.sharding import PartitionSpec as P

HD = 128
TICKS = 3
SCALE = 144.0 ** (-0.5)
EPS = 1e-06
NEGATIVE = -1e30


def dot_t(a, b):
    return lax.dot_general(a, b, (((1,), (1,)), ((), ())), preferred_element_type=jnp.float32)


def probabilities(queries, keys, docs):
    length = queries.shape[0]
    group = queries.shape[1] // HD
    heads = queries.reshape(length, group, HD)
    position = jnp.arange(length, dtype=jnp.int32)
    allowed = (position[:, None] >= position[None, :]) & (docs[:, None] == docs[None, :])
    scores = jnp.einsum("qgd,kd->gqk", heads, keys, preferred_element_type=jnp.float32) * SCALE
    scores = jnp.where(allowed, scores, NEGATIVE)
    row_max = jnp.max(scores, axis=-1, keepdims=True)
    expsum = jnp.exp(scores - row_max)
    return expsum / jnp.sum(expsum, axis=-1, keepdims=True)


def score_grads(chance, chance_low, grad_out, queries, keys, values):
    length = queries.shape[0]
    group = queries.shape[1] // HD
    query_heads = queries.reshape(length, group, HD)
    grad_heads = grad_out.reshape(length, group, HD)
    attended = jnp.einsum("gqk,kd->gqd", chance_low, values, preferred_element_type=jnp.float32)
    row_dot = jnp.sum(jnp.transpose(grad_heads, (1, 0, 2)).astype(jnp.float32) * attended, axis=-1)
    grad_chance = jnp.einsum("qgd,kd->gqk", grad_heads, values, preferred_element_type=jnp.float32)
    grad_scores = (chance * (grad_chance - row_dot[..., None])).astype(jnp.bfloat16)
    grad_query = (
        jnp.einsum("gqk,kd->qgd", grad_scores, keys, preferred_element_type=jnp.float32) * SCALE
    ).astype(jnp.bfloat16)
    grad_key = (
        jnp.einsum("gqk,qgd->kd", grad_scores, query_heads, preferred_element_type=jnp.float32)
        * SCALE
    ).astype(jnp.bfloat16)
    return grad_query.reshape(length, -1), grad_key


def on_device(cot_in, saved_inputs, queries, keys, values, docs, plan, w_value, w_out, norm_gain):
    phases = lax.axis_size("section")
    members = lax.axis_size("tensor")
    chips = members // 2
    rows, width = cot_in.shape
    half = width // 2
    length = rows * members
    rank = lax.axis_index("tensor")
    core = rank % 2
    same_core = [[2 * z + c for z in range(chips)] for c in range(2)]
    swap_pairs = [(t, t ^ 1) for t in range(members)]
    cross_pairs = [
        (s * members + t, ((s - 1) % phases) * members + (t ^ 1))
        for s in range(phases)
        for t in range(members)
    ]

    def swap(block):
        return lax.ppermute(block, "tensor", swap_pairs)

    def back(block):
        return lax.ppermute(block, "section", [(s, (s - 1) % phases) for s in range(phases)])

    def cross(block):
        return lax.ppermute(block, ("section", "tensor"), cross_pairs)

    def halves(block, axis):
        low, high = jnp.split(block, 2, axis=axis)
        return jnp.where(core == 0, low, high), jnp.where(core == 0, high, low)

    def in_order(own, other, axis):
        return jnp.where(
            core == 0,
            jnp.concatenate([own, other], axis=axis),
            jnp.concatenate([other, own], axis=axis),
        )

    def gather(block):
        spread = jnp.broadcast_to(block[None], (chips,) + block.shape)
        found = lax.all_to_all(spread, "tensor", 0, 0, axis_index_groups=same_core)
        return found.reshape(length, half)

    value_own, value_away = halves(w_value[:, 0], 1)
    value_pair = swap(value_away)
    cot_own, cot_other = halves(cot_in, 1)
    block = in_order(cot_own, swap(cot_other), 0)
    query_list = []
    key_list = []
    for tick in range(TICKS):
        chosen = plan[tick, 0]
        out_own, out_other = halves(
            lax.dynamic_index_in_dim(w_out[:, 0], chosen, 0, keepdims=False), 1
        )
        gain_own, gain_other = halves(
            lax.dynamic_index_in_dim(norm_gain[:, 0], chosen, 0, keepdims=False).astype(jnp.float32), 0
        )
        wv_own = lax.dynamic_index_in_dim(value_own, chosen, 0, keepdims=False)
        wv_pair = lax.dynamic_index_in_dim(value_pair, chosen, 0, keepdims=False)
        input_own, input_other = halves(saved_inputs[tick].astype(jnp.float32), 1)
        square = jnp.sum(input_own * input_own, -1, keepdims=True) + jnp.sum(
            input_other * input_other, -1, keepdims=True
        )
        inverse = lax.rsqrt(square / width + EPS)
        chance = probabilities(queries[tick], keys[tick], docs[tick, 0])
        chance_low = chance.astype(jnp.bfloat16)

        whole_own = gather(block)
        whole_other = swap(whole_own)
        grad_out = (dot_t(whole_own, out_own) + dot_t(whole_other, out_other)).astype(jnp.bfloat16)
        grad_heads = grad_out.reshape(length, -1, HD)
        grad_value = jnp.einsum(
            "gqk,qgd->kd", chance_low, grad_heads, preferred_element_type=jnp.float32
        ).astype(jnp.bfloat16)
        pair_value = swap(grad_value)
        partial = (dot_t(grad_value, wv_own) + dot_t(pair_value, wv_pair)).astype(jnp.bfloat16)
        terms = lax.all_to_all(
            partial.reshape(chips, 2 * rows, half), "tensor", 0, 0, axis_index_groups=same_core
        )
        summed = jnp.sum(terms.astype(jnp.float32), axis=0)
        sum_own, sum_away = halves(summed, 0)
        sum_other = swap(sum_away)
        grad_query, grad_key = score_grads(
            chance, chance_low, grad_out, queries[tick], keys[tick], values[tick]
        )
        query_list.append(grad_query)
        key_list.append(grad_key)

        scaled_own = sum_own * gain_own
        scaled_other = sum_other * gain_other
        inner = (
            jnp.sum(scaled_own * input_own, -1, keepdims=True)
            + jnp.sum(scaled_other * input_other, -1, keepdims=True)
        ) / width
        cubed = inverse * inverse * inverse * inner
        new_own = (
            cot_own.astype(jnp.float32) + inverse * scaled_own - input_own * cubed
        ).astype(jnp.bfloat16)
        new_other = (
            cot_other.astype(jnp.float32) + inverse * scaled_other - input_other * cubed
        ).astype(jnp.bfloat16)
        cot_own = back(new_own)
        cot_other = back(new_other)
        if tick < TICKS - 1:
            block = in_order(cot_own, cross(new_other), 0)
    return (in_order(cot_own, cot_other, 1), jnp.stack(query_list), jnp.stack(key_list))


def solution(mesh):
    return jax.shard_map(
        on_device,
        mesh=mesh,
        in_specs=(
            P(("section", "tensor"), None),
            P(None, ("section", "tensor"), None),
            P(None, "section", "tensor"),
            P(None, "section", "tensor"),
            P(None, "section", "tensor"),
            P(None, "section", None),
            P(None, "section"),
            P(None, "section", None, "tensor"),
            P(None, "section", "tensor", None),
            P(None, "section", None),
        ),
        out_specs=(
            P(("section", "tensor"), None),
            P(None, "section", "tensor"),
            P(None, "section", "tensor"),
        ),
        check_vma=False,
    )
```

```python
import jax
import jax.numpy as jnp
from jax import lax
from jax.sharding import PartitionSpec as P

HD = 128
TICKS = 3
SCALE = 144.0 ** (-0.5)
EPS = 1e-06
NEGATIVE = -1e30


def dot_t(a, b):
    return lax.dot_general(a, b, (((1,), (1,)), ((), ())), preferred_element_type=jnp.float32)


def probabilities(queries, keys, docs):
    length = queries.shape[0]
    group = queries.shape[1] // HD
    heads = queries.reshape(length, group, HD)
    position = jnp.arange(length, dtype=jnp.int32)
    allowed = (position[:, None] >= position[None, :]) & (docs[:, None] == docs[None, :])
    scores = jnp.einsum("qgd,kd->gqk", heads, keys, preferred_element_type=jnp.float32) * SCALE
    scores = jnp.where(allowed, scores, NEGATIVE)
    row_max = jnp.max(scores, axis=-1, keepdims=True)
    expsum = jnp.exp(scores - row_max)
    return expsum / jnp.sum(expsum, axis=-1, keepdims=True)


def score_grads(chance, chance_low, grad_out, queries, keys, values):
    length = queries.shape[0]
    group = queries.shape[1] // HD
    query_heads = queries.reshape(length, group, HD)
    grad_heads = grad_out.reshape(length, group, HD)
    attended = jnp.einsum("gqk,kd->gqd", chance_low, values, preferred_element_type=jnp.float32)
    row_dot = jnp.sum(jnp.transpose(grad_heads, (1, 0, 2)).astype(jnp.float32) * attended, axis=-1)
    grad_chance = jnp.einsum("qgd,kd->gqk", grad_heads, values, preferred_element_type=jnp.float32)
    grad_scores = (chance * (grad_chance - row_dot[..., None])).astype(jnp.bfloat16)
    grad_query = (
        jnp.einsum("gqk,kd->qgd", grad_scores, keys, preferred_element_type=jnp.float32) * SCALE
    ).astype(jnp.bfloat16)
    grad_key = (
        jnp.einsum("gqk,qgd->kd", grad_scores, query_heads, preferred_element_type=jnp.float32)
        * SCALE
    ).astype(jnp.bfloat16)
    return grad_query.reshape(length, -1), grad_key


def on_device(cot_in, saved_inputs, queries, keys, values, docs, plan, w_value, w_out, norm_gain):
    phases = lax.axis_size("section")
    members = lax.axis_size("tensor")
    rows, width = cot_in.shape
    half = width // 2
    length = rows * members
    core = lax.axis_index("tensor") % 2
    swap_pairs = [(t, t ^ 1) for t in range(members)]
    back_pairs = [(s, (s - 1) % phases) for s in range(phases)]

    def swap(block):
        return lax.ppermute(block, "tensor", swap_pairs)

    def halves(block, axis):
        low, high = jnp.split(block, 2, axis=axis)
        return jnp.where(core == 0, low, high), jnp.where(core == 0, high, low)

    def gather(block):
        both = jnp.stack(jnp.split(block, 2, axis=1))
        spread = jnp.broadcast_to(both[None], (members // 2,) + both.shape)
        found = lax.all_to_all(spread.reshape(members, rows, half), "tensor", 0, 0)
        return found.reshape(length, half)

    def scatter(partial):
        terms = lax.all_to_all(partial.reshape(members, rows, half), "tensor", 0, 0)
        terms = terms.reshape(members // 2, 2, rows, half).astype(jnp.float32)
        low, high = jnp.sum(terms[:, 0], axis=0), jnp.sum(terms[:, 1], axis=0)
        return jnp.concatenate([low, high], axis=1)

    current = cot_in
    value_own, value_away = halves(w_value[:, 0], 1)
    value_pair = swap(value_away)
    query_list = []
    key_list = []
    for tick in range(TICKS):
        chosen = plan[tick, 0]
        out_own, out_other = halves(
            lax.dynamic_index_in_dim(w_out[:, 0], chosen, 0, keepdims=False), 1
        )
        gain_row = lax.dynamic_index_in_dim(norm_gain[:, 0], chosen, 0, keepdims=False)
        wv_own = lax.dynamic_index_in_dim(value_own, chosen, 0, keepdims=False)
        wv_pair = lax.dynamic_index_in_dim(value_pair, chosen, 0, keepdims=False)
        inputs = saved_inputs[tick].astype(jnp.float32)
        inverse = lax.rsqrt(jnp.mean(inputs * inputs, -1, keepdims=True) + EPS)
        chance = probabilities(queries[tick], keys[tick], docs[tick, 0])
        chance_low = chance.astype(jnp.bfloat16)

        whole_own = gather(current)
        whole_other = swap(whole_own)
        grad_out = (dot_t(whole_own, out_own) + dot_t(whole_other, out_other)).astype(jnp.bfloat16)
        grad_heads = grad_out.reshape(length, -1, HD)
        grad_value = jnp.einsum(
            "gqk,qgd->kd", chance_low, grad_heads, preferred_element_type=jnp.float32
        ).astype(jnp.bfloat16)
        pair_value = swap(grad_value)
        partial = (dot_t(grad_value, wv_own) + dot_t(pair_value, wv_pair)).astype(jnp.bfloat16)
        summed = scatter(partial)
        grad_query, grad_key = score_grads(
            chance, chance_low, grad_out, queries[tick], keys[tick], values[tick]
        )
        query_list.append(grad_query)
        key_list.append(grad_key)

        scaled = summed * gain_row.astype(jnp.float32)
        inner = jnp.mean(scaled * inputs, -1, keepdims=True)
        updated = (
            current.astype(jnp.float32)
            + inverse * scaled
            - inputs * (inverse * inverse * inverse * inner)
        ).astype(jnp.bfloat16)
        current = lax.ppermute(updated, "section", back_pairs)
    return (current, jnp.stack(query_list), jnp.stack(key_list))


def solution(mesh):
    return jax.shard_map(
        on_device,
        mesh=mesh,
        in_specs=(
            P(("section", "tensor"), None),
            P(None, ("section", "tensor"), None),
            P(None, "section", "tensor"),
            P(None, "section", "tensor"),
            P(None, "section", "tensor"),
            P(None, "section", None),
            P(None, "section"),
            P(None, "section", None, "tensor"),
            P(None, "section", "tensor", None),
            P(None, "section", None),
        ),
        out_specs=(
            P(("section", "tensor"), None),
            P(None, "section", "tensor"),
            P(None, "section", "tensor"),
        ),
        check_vma=False,
    )
```

```python
import functools

import jax
import jax.numpy as jnp
from jax import lax
from jax.experimental import pallas as pl
from jax.experimental.pallas import tpu as pltpu
from jax.sharding import PartitionSpec as P

HD = 128
TICKS = 3
SCALE = 144.0 ** (-0.5)
EPS = 1e-06
NEGATIVE = -1e30
BIG = 56
VMEM = pl.BlockSpec(memory_space=pltpu.VMEM)


def dot_t(a, b):
    return lax.dot_general(a, b, (((1,), (1,)), ((), ())), preferred_element_type=jnp.float32)


def dot_n(a, b):
    return lax.dot_general(a, b, (((1,), (0,)), ((), ())), preferred_element_type=jnp.float32)


def token_order(place, rank, rows, chips, direction):
    length = 2 * rows * chips
    half, size, far = length // 2, 2 * rows, chips // 2
    chip, own = rank // 2, rank % 2
    core = jnp.where(place < half, own, 1 - own)
    inner = jnp.where(place < half, place, place - half)
    part = inner // size
    within = inner - part * size
    near = (chip + direction * (1 - 2 * core) * (far - 1 - part) + chips) % chips
    near_token = near * size + within
    edge = jnp.where(within < rows, (chip + far) % chips, chip)
    edge_token = edge * size + rows * core + jnp.where(within < rows, within, within - rows)
    return jnp.where(part < far - 1, near_token, edge_token)


def softmax_kernel(rows, chips, tick, q_ref, k_ref, docs_ref, gate_ref, chance_ref, low_t_ref):
    length = q_ref.shape[1]
    rank = lax.axis_index("tensor")
    down = lax.broadcasted_iota(jnp.int32, (length, length), 0)
    across = lax.broadcasted_iota(jnp.int32, (length, length), 1)
    line = docs_ref[tick]
    column = jnp.sum(jnp.where(down == across, line, 0), axis=1, keepdims=True)
    allowed = (down >= across) & (column == line)
    key_hot = (token_order(down, rank, rows, chips, 1) == across).astype(jnp.bfloat16)
    query_hot = (token_order(across, rank, rows, chips, -1) == down).astype(jnp.bfloat16)
    for head in range(q_ref.shape[2] // HD):
        scores = dot_t(q_ref[tick, :, head * HD : (head + 1) * HD], k_ref[tick]) * SCALE
        scores = jnp.where(allowed, scores, NEGATIVE)
        expsum = jnp.exp(scores - jnp.max(scores, axis=-1, keepdims=True))
        chance = expsum / jnp.sum(expsum, axis=-1, keepdims=True)
        chance_ref[head] = chance
        turned = dot_t(key_hot, chance.astype(jnp.bfloat16)).astype(jnp.bfloat16)
        low_t_ref[head] = dot_n(turned, query_hot).astype(jnp.bfloat16)


def grads_kernel(rows, chips, tick, chance_ref, go_ref, q_ref, k_ref, v_ref, gq_ref, gk_ref):
    length = q_ref.shape[1]
    rank = lax.axis_index("tensor")
    down = lax.broadcasted_iota(jnp.int32, (length, length), 0)
    across = lax.broadcasted_iota(jnp.int32, (length, length), 1)
    query_hot = (token_order(across, rank, rows, chips, -1) == down).astype(jnp.bfloat16)
    grad_out = dot_n(query_hot, go_ref[...]).astype(jnp.bfloat16)
    total = jnp.zeros(gk_ref.shape, jnp.float32)
    for head in range(q_ref.shape[2] // HD):
        columns = slice(head * HD, (head + 1) * HD)
        chance = chance_ref[head]
        grad = grad_out[:, columns]
        attended = dot_n(chance.astype(jnp.bfloat16), v_ref[tick])
        row_dot = jnp.sum(grad.astype(jnp.float32) * attended, axis=-1, keepdims=True)
        grad_chance = dot_t(grad, v_ref[tick])
        grad_scores = (chance * (grad_chance - row_dot)).astype(jnp.bfloat16)
        gq_ref[:, columns] = (dot_n(grad_scores, k_ref[tick]) * SCALE).astype(jnp.bfloat16)
        total = total + lax.dot_general(
            grad_scores,
            q_ref[tick, :, columns],
            (((0,), (0,)), ((), ())),
            preferred_element_type=jnp.float32,
        )
    gk_ref[...] = (total * SCALE).astype(jnp.bfloat16)


def order_kernel(a_ref, b_ref, pair_ref):
    rows = a_ref.shape[0]
    first = lax.axis_index("tensor") % 2 == 0
    pair_ref[:rows] = jnp.where(first, a_ref[...], b_ref[...])
    pair_ref[rows:] = jnp.where(first, b_ref[...], a_ref[...])


def out_kernel(*refs):
    *parts, here_ref, own_ref, pair_ref, keep_ref, send_ref, mine_ref = refs
    at = 0
    for part in parts:
        mine_ref[at : at + part.shape[0]] = part[...]
        at += part.shape[0]
    rows = here_ref.shape[0] // 2
    first = lax.axis_index("tensor") % 2 == 0
    mine_ref[at:] = jnp.where(first, here_ref[:rows], here_ref[rows:])
    keep_ref[...] = dot_t(mine_ref[...], own_ref[...]).astype(jnp.bfloat16)
    send_ref[...] = dot_t(mine_ref[...], pair_ref[...]).astype(jnp.bfloat16)


def value_kernel(keep_ref, recv_ref, low_t_ref, go_ref, own_ref, away_ref):
    half = keep_ref.shape[0]
    go_ref[:half] = keep_ref[...]
    go_ref[half:] = recv_ref[...]
    total = jnp.zeros((2 * half, HD), jnp.float32)
    for head in range(low_t_ref.shape[0]):
        total = total + dot_n(low_t_ref[head], go_ref[:, head * HD : (head + 1) * HD])
    total = total.astype(jnp.bfloat16)
    own_ref[...] = total[:half]
    away_ref[...] = total[half:]


def partial_kernel(gv_ref, gv_pair_ref, own_ref, pair_ref, *outs):
    total = dot_t(gv_ref[...], own_ref[...]) + dot_t(gv_pair_ref[...], pair_ref[...])
    total = total.astype(jnp.bfloat16)
    at = 0
    for out in outs:
        out[...] = total[at : at + out.shape[0]]
        at += out.shape[0]


def sum_kernel(*refs):
    *near, away_ref, here_ref, total_ref = refs
    rows = away_ref.shape[0]
    total = near[0][...].astype(jnp.float32)
    for ref in near[1:]:
        total = total + ref[...].astype(jnp.float32)
    edge = away_ref[...].astype(jnp.float32) + here_ref[...].astype(jnp.float32)
    first = lax.axis_index("tensor") % 2 == 0
    total_ref[:rows] = total[:rows] + jnp.where(first, edge, 0.0)
    total_ref[rows:] = total[rows:] + jnp.where(first, 0.0, edge)


def norm_kernel(tick, a_ref, b_ref, x_own_ref, x_other_ref, gain_ref, current_ref, new_ref, mine_ref):
    rows = x_own_ref.shape[1]
    first = lax.axis_index("tensor") % 2 == 0
    gain = gain_ref[...].astype(jnp.float32)
    low = jnp.where(first, x_own_ref[tick], x_other_ref[tick])
    high = jnp.where(first, x_other_ref[tick], x_own_ref[tick])
    found = []
    for at, piece in ((0, low), (rows, high)):
        inputs = piece.astype(jnp.float32)
        inverse = lax.rsqrt(jnp.mean(inputs * inputs, -1, keepdims=True) + EPS)
        scaled = (a_ref[at : at + rows] + b_ref[at : at + rows]) * gain
        inner = jnp.mean(scaled * inputs, -1, keepdims=True)
        updated = (
            current_ref[at : at + rows].astype(jnp.float32)
            + inverse * scaled
            - inputs * (inverse * inverse * inverse * inner)
        ).astype(jnp.bfloat16)
        new_ref[at : at + rows] = updated
        found.append(updated)
    mine_ref[...] = jnp.where(first, found[0], found[1])


def choose_kernel(tick, plan_ref, *refs):
    chosen = plan_ref[tick, 0]
    count = (len(refs) - 2) // 2
    sources, outs, sems = refs[:count], refs[count + 1 : -1], refs[-1]
    copies = [
        pltpu.make_async_copy(source.at[chosen, 0] if source.ndim == 4 else source.at[chosen], out, sems.at[i])
        for i, (source, out) in enumerate(zip(sources, outs))
    ]
    for copy in copies:
        copy.start()
    for copy in copies:
        copy.wait()


def on_core(kernel, shapes, operands, scratch=(), limit=24, gate=None):
    specs = [VMEM] * len(operands)
    if gate is not None:
        specs.append(pl.BlockSpec(memory_space=pl.ANY))
        operands = (*operands, gate)
    return pl.pallas_call(
        kernel,
        out_shape=shapes,
        in_specs=specs,
        out_specs=[VMEM] * len(shapes),
        scratch_shapes=list(scratch),
        cost_estimate=pl.CostEstimate(flops=1000, bytes_accessed=1000, transcendentals=0),
        compiler_params=pltpu.CompilerParams(vmem_limit_bytes=limit * 1024 * 1024),
    )(*operands)


def choose(tick, plan, weights, gate):
    anywhere = pl.BlockSpec(memory_space=pl.ANY)
    shapes = [jax.ShapeDtypeStruct(item.shape[-2:], item.dtype) for item in weights]
    return pl.pallas_call(
        functools.partial(choose_kernel, tick),
        out_shape=shapes,
        in_specs=[pl.BlockSpec(memory_space=pltpu.SMEM)] + [anywhere] * (len(weights) + 1),
        out_specs=[VMEM] * len(shapes),
        scratch_shapes=[pltpu.SemaphoreType.DMA((len(weights),))],
        cost_estimate=pl.CostEstimate(flops=1000, bytes_accessed=1000, transcendentals=0),
        compiler_params=pltpu.CompilerParams(vmem_limit_bytes=24 * 1024 * 1024),
    )(plan, *weights, gate)


def bf16(*shape):
    return jax.ShapeDtypeStruct(shape, jnp.bfloat16)


def f32(*shape):
    return jax.ShapeDtypeStruct(shape, jnp.float32)


def on_device(cot_in, saved_inputs, queries, keys, values, docs, plan, w_value, w_out, norm_gain):
    phases = lax.axis_size("section")
    members = lax.axis_size("tensor")
    chips = members // 2
    far = chips // 2
    rows, width = cot_in.shape
    length = rows * members
    half = length // 2
    heads = queries.shape[2] // HD
    hold = lax.optimization_barrier

    def swap(block):
        return lax.ppermute(block, "tensor", [(t, t ^ 1) for t in range(members)])

    def along(block, by):
        return lax.ppermute(block, "section", [(s, (s + by) % phases) for s in range(phases)])

    def hop(block, steps, back):
        pairs = []
        for s in range(phases):
            for z in range(chips):
                for c in range(2):
                    there = (z + (steps if c == 0 else -steps)) % chips
                    target = (s - back) % phases
                    pairs.append((s * members + 2 * z + c, target * members + 2 * there + c))
        return lax.ppermute(block, ("section", "tensor"), pairs)

    def attention_ready(tick, gate):
        return on_core(
            functools.partial(softmax_kernel, rows, chips, tick),
            [f32(heads, length, length), bf16(heads, length, length)],
            (queries, keys, docs),
            limit=BIG,
            gate=gate,
        )

    def grads(chance, grad_out, tick):
        return on_core(
            functools.partial(grads_kernel, rows, chips, tick),
            [bf16(*queries.shape[1:]), bf16(*keys.shape[1:])],
            (chance, grad_out, queries, keys, values),
            limit=BIG,
        )

    def gather(pair, mine, back, done):
        near = [hop(pair, k, back) for k in range(far - 1, 0, -1)]
        away = hop(mine, far, back)
        here = hop(pair, 0, back) if back else pair
        return hold((near + [away, here], done))

    def scatter(blocks, done):
        steps = list(range(far - 1, 0, -1)) + [far]
        moved = [hop(block, k, 0) for block, k in zip(blocks[:-1], steps)]
        moved, done = hold((moved + [blocks[-1]], done))
        total = on_core(sum_kernel, [f32(2 * rows, width)], moved)[0]
        return total, swap(total), done

    current = on_core(order_kernel, [bf16(2 * rows, width)], (cot_in, swap(cot_in)))[0]
    current, *later = hold((current, w_out, w_value, saved_inputs))
    away_out, away_value, inputs_away = (swap(item) for item in later)
    weights = [w_out, w_value, away_out, away_value, norm_gain]
    mine = cot_in
    query_list = []
    key_list = []
    for tick in range(TICKS):
        last = tick == TICKS - 1
        if tick == 0:
            done = attention_ready(0, current), choose(0, plan, weights, current), inputs_away
        elif tick == 1:
            done = attention_ready(2, current)
        else:
            done = ()
        parts, done = gather(current, mine, 1 if tick else 0, done)
        if tick == 0:
            ready, chosen, inputs_away = done
        elif tick == 1:
            ready_last = done
        current = parts[-1]
        chance, low_t = ready
        keep, send = on_core(
            out_kernel,
            [bf16(half, heads * HD)] * 2,
            parts + [chosen[0], chosen[2]],
            [pltpu.VMEM((half, width), jnp.bfloat16)],
        )
        grad_out, value_keep, value_send = on_core(
            value_kernel,
            [bf16(length, heads * HD), bf16(half, HD), bf16(half, HD)],
            (keep, swap(send), low_t),
        )
        blocks = on_core(
            partial_kernel,
            [bf16(2 * rows, width)] * (far - 1) + [bf16(rows, width)] * 2,
            (value_keep, swap(value_send), chosen[1], chosen[3]),
        )
        found = grads(chance, grad_out, tick)
        if last:
            done = jnp.stack(query_list + [found[0]]), jnp.stack(key_list + [found[1]])
        else:
            done = found, choose(tick + 1, plan, weights, blocks[-1])
            if tick == 0:
                done += (attention_ready(1, blocks[-1]),)
        total, total_pair, done = scatter(blocks, done)
        gain = chosen[4]
        if last:
            query, key = done
        else:
            found, chosen = done[:2]
            query_list.append(found[0])
            key_list.append(found[1])
            ready = done[2] if tick == 0 else ready_last
        current, mine = on_core(
            functools.partial(norm_kernel, tick),
            [bf16(2 * rows, width), bf16(rows, width)],
            (total, total_pair, saved_inputs, inputs_away, gain, current),
        )
    return along(mine, -1), query, key


def solution(mesh):
    return jax.shard_map(
        on_device,
        mesh=mesh,
        in_specs=(
            P(("section", "tensor"), None),
            P(None, ("section", "tensor"), None),
            P(None, "section", "tensor"),
            P(None, "section", "tensor"),
            P(None, "section", "tensor"),
            P(None, "section", None),
            P(None, "section"),
            P(None, "section", None, "tensor"),
            P(None, "section", "tensor", None),
            P(None, "section", None),
        ),
        out_specs=(
            P(("section", "tensor"), None),
            P(None, "section", "tensor"),
            P(None, "section", "tensor"),
        ),
        check_vma=False,
    )
```

```python
import functools

import jax
import jax.numpy as jnp
from jax import lax
from jax.experimental import pallas as pl
from jax.experimental.pallas import tpu as pltpu
from jax.sharding import PartitionSpec as P

HD = 128
TICKS = 3
SCALE = 144.0 ** (-0.5)
EPS = 1e-06
NEGATIVE = -1e30
VMEM = pl.BlockSpec(memory_space=pltpu.VMEM)


def dot_t(a, b):
    return lax.dot_general(a, b, (((1,), (1,)), ((), ())), preferred_element_type=jnp.float32)


def dot_n(a, b):
    return lax.dot_general(a, b, (((1,), (0,)), ((), ())), preferred_element_type=jnp.float32)


def token_order(place, rank, rows, chips, direction):
    length = 2 * rows * chips
    half, size, far = length // 2, 2 * rows, chips // 2
    chip, own = rank // 2, rank % 2
    core = jnp.where(place < half, own, 1 - own)
    inner = jnp.where(place < half, place, place - half)
    part = inner // size
    within = inner - part * size
    near = (chip + direction * (1 - 2 * core) * (far - part) + chips) % chips
    edge = jnp.where(core == 0, (chip + far) % chips, chip)
    return jnp.where(part == 0, edge, near) * size + within


def softmax_kernel(rows, chips, wait, q_ref, k_ref, docs_ref, chance_ref, low_t_ref):
    length = q_ref.shape[0]
    rank = lax.axis_index("tensor")
    down = lax.broadcasted_iota(jnp.int32, (length, length), 0)
    across = lax.broadcasted_iota(jnp.int32, (length, length), 1)
    key_hot = (token_order(down, rank, rows, chips, 1) == across).astype(jnp.bfloat16)
    query_hot = (token_order(across, rank, rows, chips, -1) == down).astype(jnp.bfloat16)
    wait()
    line = docs_ref[...]
    column = jnp.sum(jnp.where(down == across, line, 0), axis=1, keepdims=True)
    allowed = (down >= across) & (column == line)
    for head in range(q_ref.shape[1] // HD):
        scores = dot_t(q_ref[:, head * HD : (head + 1) * HD], k_ref[...]) * SCALE
        scores = jnp.where(allowed, scores, NEGATIVE)
        expsum = jnp.exp(scores - jnp.max(scores, axis=-1, keepdims=True))
        chance = expsum / jnp.sum(expsum, axis=-1, keepdims=True)
        chance_ref[head] = chance
        turned = dot_t(key_hot, chance.astype(jnp.bfloat16)).astype(jnp.bfloat16)
        low_t_ref[head] = dot_n(turned, query_hot).astype(jnp.bfloat16)


def grads_kernel(rows, chips, wait, chance_ref, go_ref, q_ref, k_ref, v_ref, gq_ref, gk_ref):
    length = q_ref.shape[0]
    rank = lax.axis_index("tensor")
    down = lax.broadcasted_iota(jnp.int32, (length, length), 0)
    across = lax.broadcasted_iota(jnp.int32, (length, length), 1)
    query_hot = (token_order(across, rank, rows, chips, -1) == down).astype(jnp.bfloat16)
    wait()
    grad_out = dot_n(query_hot, go_ref[...]).astype(jnp.bfloat16)
    total = jnp.zeros(gk_ref.shape, jnp.float32)
    for head in range(q_ref.shape[1] // HD):
        columns = slice(head * HD, (head + 1) * HD)
        chance = chance_ref[head]
        grad = grad_out[:, columns]
        attended = dot_n(chance.astype(jnp.bfloat16), v_ref[...])
        row_dot = jnp.sum(grad.astype(jnp.float32) * attended, axis=-1, keepdims=True)
        grad_chance = dot_t(grad, v_ref[...])
        grad_scores = (chance * (grad_chance - row_dot)).astype(jnp.bfloat16)
        gq_ref[:, columns] = (dot_n(grad_scores, k_ref[...]) * SCALE).astype(jnp.bfloat16)
        total = total + lax.dot_general(
            grad_scores,
            q_ref[:, columns],
            (((0,), (0,)), ((), ())),
            preferred_element_type=jnp.float32,
        )
    gk_ref[...] = (total * SCALE).astype(jnp.bfloat16)


def order_kernel(a_ref, b_ref, pair_ref):
    rows = a_ref.shape[0]
    first = lax.axis_index("tensor") % 2 == 0
    pair_ref[:rows] = jnp.where(first, a_ref[...], b_ref[...])
    pair_ref[rows:] = jnp.where(first, b_ref[...], a_ref[...])


def out_kernel(*refs):
    edge_ref, *near, own_ref, pair_ref, keep_ref, send_ref, mine_ref = refs
    size = edge_ref.shape[0]
    for i, part in enumerate((edge_ref, *near[::-1])):
        mine_ref[i * size : (i + 1) * size] = part[...]
    send_ref[...] = dot_t(mine_ref[...], pair_ref[...]).astype(jnp.bfloat16)
    keep_ref[...] = dot_t(mine_ref[...], own_ref[...]).astype(jnp.bfloat16)


def value_kernel(keep_ref, recv_ref, low_t_ref, go_ref, own_ref, away_ref):
    half = keep_ref.shape[0]
    go_ref[:half] = keep_ref[...]
    go_ref[half:] = recv_ref[...]
    total = jnp.zeros((2 * half, HD), jnp.float32)
    for head in range(low_t_ref.shape[0]):
        total = total + dot_n(low_t_ref[head], go_ref[:, head * HD : (head + 1) * HD])
    total = total.astype(jnp.bfloat16)
    own_ref[...] = total[:half]
    away_ref[...] = total[half:]


def partial_kernel(gv_ref, gv_pair_ref, own_ref, pair_ref, *outs):
    total = dot_t(gv_ref[...], own_ref[...]) + dot_t(gv_pair_ref[...], pair_ref[...])
    total = total.astype(jnp.bfloat16)
    size = outs[0].shape[0]
    for i, out in enumerate(outs):
        at = (i + 1) % len(outs) * size
        out[...] = total[at : at + size]


def sum_kernel(*refs):
    *parts, total_ref = refs
    total = parts[0][...].astype(jnp.float32)
    for ref in parts[1:]:
        total = total + ref[...].astype(jnp.float32)
    total_ref[...] = total


def lines_kernel(wait, own_ref, other_ref, pair_ref):
    wait()
    order_kernel(own_ref, other_ref, pair_ref)


def norm_kernel(a_ref, b_ref, x_ref, gain_ref, even_ref, odd_ref, new_ref, mine_ref):
    rows = mine_ref.shape[0]
    first = lax.axis_index("tensor") % 2 == 0
    inputs = x_ref[...].astype(jnp.float32)
    inverse = lax.rsqrt(jnp.mean(inputs * inputs, -1, keepdims=True) + EPS)
    scaled = (a_ref[...] + b_ref[...]) * gain_ref[...].astype(jnp.float32)
    inner = jnp.mean(scaled * inputs, -1, keepdims=True)
    current = jnp.where(first, even_ref[...], odd_ref[...]).astype(jnp.float32)
    updated = (
        current + inverse * scaled - inputs * (inverse * inverse * inverse * inner)
    ).astype(jnp.bfloat16)
    new_ref[...] = updated
    mine_ref[...] = jnp.where(first, updated[:rows], updated[rows:])


def staged_kernel(kernel, picks, count, *refs):
    sources = refs[: len(picks)]
    outs = refs[-count - len(picks) - 1 : -len(picks) - 1]
    held, sems = refs[-len(picks) - 1 : -1], refs[-1]
    copies = [
        pltpu.make_async_copy(source if pick is None else source.at[pick], slot, sems.at[i])
        for i, (pick, source, slot) in enumerate(zip(picks, sources, held))
    ]
    for copy in copies:
        copy.start()

    def wait():
        for copy in copies:
            copy.wait()

    kernel(wait, *held, *outs)


def choose_kernel(tick, plan_ref, *refs):
    chosen = plan_ref[tick, 0]
    count = (len(refs) - 2) // 2
    sources, outs, sems = refs[:count], refs[count + 1 : -1], refs[-1]
    copies = []
    for i, (source, out) in enumerate(zip(sources, outs)):
        view = source.at[chosen, 0] if len(source.shape) == 4 else source.at[chosen]
        copies.append(pltpu.make_async_copy(view, out, sems.at[i]))
    for copy in copies:
        copy.start()
    for copy in copies:
        copy.wait()


FAR = pl.BlockSpec(memory_space=pltpu.HBM)
LIGHT = pl.CostEstimate(flops=1000, bytes_accessed=1000, transcendentals=0)
PARAMS = pltpu.CompilerParams(vmem_limit_bytes=24 * 1024 * 1024)


def staged(kernel, shapes, operands, gate):
    arrays, picks = [pair[0] for pair in operands], [pair[1] for pair in operands]
    slots = [
        pltpu.VMEM(array.shape if pick is None else array.shape[1:], array.dtype)
        for array, pick in operands
    ]
    return pl.pallas_call(
        functools.partial(staged_kernel, kernel, picks, len(shapes)),
        out_shape=shapes,
        in_specs=[FAR] * (len(arrays) + 1),
        out_specs=[VMEM] * len(shapes),
        scratch_shapes=slots + [pltpu.SemaphoreType.DMA((len(picks),))],
        cost_estimate=LIGHT,
        compiler_params=PARAMS,
    )(*arrays, gate)


def on_core(kernel, shapes, operands, scratch=()):
    return pl.pallas_call(
        kernel,
        out_shape=shapes,
        in_specs=[VMEM] * len(operands),
        out_specs=[VMEM] * len(shapes),
        scratch_shapes=list(scratch),
        cost_estimate=LIGHT,
        compiler_params=PARAMS,
    )(*operands)


def choose(tick, plan, weights, gate):
    shapes = [jax.ShapeDtypeStruct(item.shape[-2:], item.dtype) for item in weights]
    return pl.pallas_call(
        functools.partial(choose_kernel, tick),
        out_shape=shapes,
        in_specs=[pl.BlockSpec(memory_space=pltpu.SMEM)] + [FAR] * (len(weights) + 1),
        out_specs=[VMEM] * len(shapes),
        scratch_shapes=[pltpu.SemaphoreType.DMA((len(weights),))],
        cost_estimate=LIGHT,
        compiler_params=PARAMS,
    )(plan, *weights, gate)


def bf16(*shape):
    return jax.ShapeDtypeStruct(shape, jnp.bfloat16)


def f32(*shape):
    return jax.ShapeDtypeStruct(shape, jnp.float32)


def on_device(cot_in, saved_inputs, queries, keys, values, docs, plan, w_value, w_out, norm_gain):
    phases = lax.axis_size("section")
    members = lax.axis_size("tensor")
    chips = members // 2
    far = chips // 2
    rows, width = cot_in.shape
    length = rows * members
    half = length // 2
    heads = queries.shape[2] // HD
    hold = lax.optimization_barrier

    def swap(block):
        return lax.ppermute(block, "tensor", [(t, t ^ 1) for t in range(members)])

    def along(block, by):
        return lax.ppermute(block, "section", [(s, (s + by) % phases) for s in range(phases)])

    def hop(block, steps, back):
        pairs = []
        for section in range(phases):
            for z in range(chips):
                up, down = (z + steps) % chips, (z - steps) % chips if steps != far else z
                base = (section - back) % phases * members
                pairs.append((section * members + 2 * z, base + 2 * up))
                pairs.append((section * members + 2 * z + 1, base + 2 * down + 1))
        return lax.ppermute(block, ("section", "tensor"), pairs)

    def attention_ready(tick, gate):
        return staged(
            functools.partial(softmax_kernel, rows, chips),
            [f32(heads, length, length), bf16(heads, length, length)],
            [(item, tick) for item in (queries, keys, docs)],
            gate,
        )

    def grads(chance, grad_out, tick, gate):
        return staged(
            functools.partial(grads_kernel, rows, chips),
            [bf16(*queries.shape[1:]), bf16(*keys.shape[1:])],
            [(chance, None), (grad_out, None)]
            + [(item, tick) for item in (queries, keys, values)],
            gate,
        )

    def gather(pair, back, done):
        moved = [hop(pair, k, back) for k in (far, *range(1, far))]
        return hold((moved, done))

    def scatter(blocks, done):
        steps = list(range(far - 1, 0, -1)) + [far]
        moved = [hop(block, k, 0) for block, k in zip(blocks, steps)]
        return hold((moved, done))

    other = swap(cot_in)
    other, *later = hold((other, w_value, w_out))
    away_value, away_out = (swap(item) for item in later)
    pair = on_core(order_kernel, [bf16(2 * rows, width)], (cot_in, other))[0]
    weights = [w_out, away_out, w_value, away_value, norm_gain]
    query_list = []
    key_list = []
    for tick in range(TICKS):
        last = tick == TICKS - 1
        if tick == 0:
            done = attention_ready(0, pair), choose(0, plan, weights, pair)
        elif tick == 1:
            done = attention_ready(2, pair)
        else:
            done = ()
        parts, done = gather(pair, 1 if tick else 0, done)
        if tick == 0:
            ready, chosen = done
        elif tick == 1:
            ready_last = done
        own_out, pair_out, own_value, pair_value, gain = chosen
        chance, low_t = ready
        keep, send = on_core(
            out_kernel,
            [bf16(half, heads * HD)] * 2,
            [*parts, own_out, pair_out],
            [pltpu.VMEM((half, width), jnp.bfloat16)],
        )
        grad_out, value_keep, value_send = on_core(
            value_kernel,
            [bf16(length, heads * HD), bf16(half, HD), bf16(half, HD)],
            (keep, swap(send), low_t),
        )
        blocks = on_core(
            partial_kernel,
            [bf16(2 * rows, width)] * far,
            (value_keep, swap(value_send), own_value, pair_value),
        )
        gate = blocks[-1]
        found = grads(chance, grad_out, tick, gate)
        if tick:
            even, odd = swap(parts[0]), parts[0]
        else:
            even = odd = pair
            later, _ = hold((saved_inputs, gate))
            inputs_away = swap(later)
        lines = staged(
            lines_kernel,
            [bf16(2 * rows, width)],
            [(saved_inputs, tick), (inputs_away, tick)],
            gate,
        )[0]
        if last:
            done = jnp.stack(query_list + [found[0]]), jnp.stack(key_list + [found[1]])
        elif tick == 0:
            done = found, choose(1, plan, weights, gate), attention_ready(1, gate), inputs_away
        else:
            done = found, choose(2, plan, weights, gate)
        done = done, lines, even
        terms, (done, lines, even) = scatter(blocks, done)
        total = on_core(sum_kernel, [f32(2 * rows, width)], terms)[0]
        if last:
            query, key = done
        else:
            found, chosen = done[:2]
            if tick == 0:
                ready, inputs_away = done[2:]
            else:
                ready = ready_last
            query_list.append(found[0])
            key_list.append(found[1])
        pair, mine = on_core(
            norm_kernel,
            [bf16(2 * rows, width), bf16(rows, width)],
            (total, swap(total), lines, gain, even, odd),
        )
    return along(mine, -1), query, key


def solution(mesh):
    return jax.shard_map(
        on_device,
        mesh=mesh,
        in_specs=(
            P(("section", "tensor"), None),
            P(None, ("section", "tensor"), None),
            P(None, "section", "tensor"),
            P(None, "section", "tensor"),
            P(None, "section", "tensor"),
            P(None, "section", None),
            P(None, "section"),
            P(None, "section", None, "tensor"),
            P(None, "section", "tensor", None),
            P(None, "section", None),
        ),
        out_specs=(
            P(("section", "tensor"), None),
            P(None, "section", "tensor"),
            P(None, "section", "tensor"),
        ),
        check_vma=False,
    )
```

```python
import functools

import jax
import jax.numpy as jnp
from jax import lax
from jax.experimental import pallas as pl
from jax.experimental.pallas import tpu as pltpu
from jax.sharding import PartitionSpec as P

HD = 128
TICKS = 3
SCALE = 144.0 ** (-0.5)
EPS = 1e-06
NEGATIVE = -1e30
VMEM = pl.BlockSpec(memory_space=pltpu.VMEM)


def dot_t(a, b):
    return lax.dot_general(a, b, (((1,), (1,)), ((), ())), preferred_element_type=jnp.float32)


def dot_n(a, b):
    return lax.dot_general(a, b, (((1,), (0,)), ((), ())), preferred_element_type=jnp.float32)


def token_order(place, rank, rows, chips, direction):
    length = 2 * rows * chips
    half, size, far = length // 2, 2 * rows, chips // 2
    chip, own = rank // 2, rank % 2
    core = jnp.where(place < half, own, 1 - own)
    inner = jnp.where(place < half, place, place - half)
    part = inner // size
    within = inner - part * size
    near = (chip + direction * (1 - 2 * core) * (far - part) + chips) % chips
    edge = jnp.where(core == 0, (chip + far) % chips, chip)
    return jnp.where(part == 0, edge, near) * size + within


def softmax_kernel(rows, chips, wait, q_ref, k_ref, docs_ref, chance_ref, low_t_ref):
    length = q_ref.shape[0]
    rank = lax.axis_index("tensor")
    down = lax.broadcasted_iota(jnp.int32, (length, length), 0)
    across = lax.broadcasted_iota(jnp.int32, (length, length), 1)
    key_hot = (token_order(down, rank, rows, chips, 1) == across).astype(jnp.bfloat16)
    query_hot = (token_order(across, rank, rows, chips, -1) == down).astype(jnp.bfloat16)
    wait()
    line = docs_ref[...]
    column = jnp.sum(jnp.where(down == across, line, 0), axis=1, keepdims=True)
    allowed = (down >= across) & (column == line)
    for head in range(q_ref.shape[1] // HD):
        scores = dot_t(q_ref[:, head * HD : (head + 1) * HD], k_ref[...]) * SCALE
        scores = jnp.where(allowed, scores, NEGATIVE)
        expsum = jnp.exp(scores - jnp.max(scores, axis=-1, keepdims=True))
        chance = expsum / jnp.sum(expsum, axis=-1, keepdims=True)
        chance_ref[head] = chance
        turned = dot_t(key_hot, chance.astype(jnp.bfloat16)).astype(jnp.bfloat16)
        low_t_ref[head] = dot_n(turned, query_hot).astype(jnp.bfloat16)


def grads_kernel(rows, chips, wait, chance_ref, go_ref, q_ref, k_ref, v_ref, gq_ref, gk_ref):
    length = q_ref.shape[0]
    rank = lax.axis_index("tensor")
    down = lax.broadcasted_iota(jnp.int32, (length, length), 0)
    across = lax.broadcasted_iota(jnp.int32, (length, length), 1)
    query_hot = (token_order(across, rank, rows, chips, -1) == down).astype(jnp.bfloat16)
    wait()
    grad_out = dot_n(query_hot, go_ref[...]).astype(jnp.bfloat16)
    total = jnp.zeros(gk_ref.shape, jnp.float32)
    for head in range(q_ref.shape[1] // HD):
        columns = slice(head * HD, (head + 1) * HD)
        chance = chance_ref[head]
        grad = grad_out[:, columns]
        attended = dot_n(chance.astype(jnp.bfloat16), v_ref[...])
        row_dot = jnp.sum(grad.astype(jnp.float32) * attended, axis=-1, keepdims=True)
        grad_chance = dot_t(grad, v_ref[...])
        grad_scores = (chance * (grad_chance - row_dot)).astype(jnp.bfloat16)
        gq_ref[:, columns] = (dot_n(grad_scores, k_ref[...]) * SCALE).astype(jnp.bfloat16)
        total = total + lax.dot_general(
            grad_scores,
            q_ref[:, columns],
            (((0,), (0,)), ((), ())),
            preferred_element_type=jnp.float32,
        )
    gk_ref[...] = (total * SCALE).astype(jnp.bfloat16)


def order_kernel(a_ref, b_ref, pair_ref):
    rows = a_ref.shape[0]
    first = lax.axis_index("tensor") % 2 == 0
    pair_ref[:rows] = jnp.where(first, a_ref[...], b_ref[...])
    pair_ref[rows:] = jnp.where(first, b_ref[...], a_ref[...])


def out_kernel(*refs):
    *parts, own_ref, pair_ref, keep_ref, send_ref, mine_ref = refs
    size = parts[0].shape[0]
    for i, part in enumerate(parts):
        mine_ref[i * size : (i + 1) * size] = part[...]
    send_ref[...] = dot_t(mine_ref[...], pair_ref[...]).astype(jnp.bfloat16)
    keep_ref[...] = dot_t(mine_ref[...], own_ref[...]).astype(jnp.bfloat16)


def value_kernel(keep_ref, recv_ref, low_t_ref, go_ref, own_ref, away_ref):
    half = keep_ref.shape[0]
    go_ref[:half] = keep_ref[...]
    go_ref[half:] = recv_ref[...]
    total = jnp.zeros((2 * half, HD), jnp.float32)
    for head in range(low_t_ref.shape[0]):
        total = total + dot_n(low_t_ref[head], go_ref[:, head * HD : (head + 1) * HD])
    total = total.astype(jnp.bfloat16)
    own_ref[...] = total[:half]
    away_ref[...] = total[half:]


def partial_kernel(gv_ref, gv_pair_ref, own_ref, pair_ref, *outs):
    total = dot_t(gv_ref[...], own_ref[...]) + dot_t(gv_pair_ref[...], pair_ref[...])
    total = total.astype(jnp.bfloat16)
    size = outs[0].shape[0]
    for i, out in enumerate(outs):
        at = (len(outs) - 1 - i) * size
        out[...] = total[at : at + size]


def add_kernel(own_ref, relayed_ref, total_ref):
    first = lax.axis_index("tensor") % 2 == 0
    own = own_ref[...].astype(jnp.float32)
    relayed = relayed_ref[...].astype(jnp.float32)
    total_ref[...] = (own + jnp.where(first, relayed, 0.0)).astype(jnp.bfloat16)


def sum_kernel(*refs):
    *near, edge_ref, total_ref = refs
    first = lax.axis_index("tensor") % 2 == 0
    total = jnp.where(first, 0.0, edge_ref[...].astype(jnp.float32))
    for ref in near:
        total = total + ref[...].astype(jnp.float32)
    total_ref[...] = total.astype(total_ref.dtype)


def lines_kernel(wait, own_ref, other_ref, pair_ref):
    wait()
    order_kernel(own_ref, other_ref, pair_ref)


def norm_kernel(a_ref, b_ref, x_ref, gain_ref, even_ref, odd_ref, new_ref, mine_ref):
    rows = mine_ref.shape[0]
    first = lax.axis_index("tensor") % 2 == 0
    inputs = x_ref[...].astype(jnp.float32)
    inverse = lax.rsqrt(jnp.mean(inputs * inputs, -1, keepdims=True) + EPS)
    scaled = a_ref[...].astype(jnp.float32) + b_ref[...].astype(jnp.float32)
    scaled = scaled * gain_ref[...].astype(jnp.float32)
    inner = jnp.mean(scaled * inputs, -1, keepdims=True)
    current = jnp.where(first, even_ref[...], odd_ref[...]).astype(jnp.float32)
    updated = (
        current + inverse * scaled - inputs * (inverse * inverse * inverse * inner)
    ).astype(jnp.bfloat16)
    new_ref[...] = updated
    mine_ref[...] = jnp.where(first, updated[:rows], updated[rows:])


def staged_kernel(kernel, picks, count, *refs):
    sources = refs[: len(picks)]
    outs = refs[-count - len(picks) - 1 : -len(picks) - 1]
    held, sems = refs[-len(picks) - 1 : -1], refs[-1]
    copies = [
        pltpu.make_async_copy(source if pick is None else source.at[pick], slot, sems.at[i])
        for i, (pick, source, slot) in enumerate(zip(picks, sources, held))
    ]
    for copy in copies:
        copy.start()

    def wait():
        for copy in copies:
            copy.wait()

    kernel(wait, *held, *outs)


def choose_kernel(tick, plan_ref, *refs):
    chosen = plan_ref[tick, 0]
    count = (len(refs) - 3) // 2
    sources, outs, mark, sems = refs[:count], refs[count + 1 : -2], refs[-2], refs[-1]
    mark[...] = jnp.zeros_like(mark)
    copies = []
    for i, (source, out) in enumerate(zip(sources, outs)):
        view = source.at[chosen, 0] if len(source.shape) == 4 else source.at[chosen]
        copies.append(pltpu.make_async_copy(view, out, sems.at[i]))
    for copy in copies:
        copy.start()
    for copy in copies:
        copy.wait()


FAR = pl.BlockSpec(memory_space=pltpu.HBM)
LIGHT = pl.CostEstimate(flops=1000, bytes_accessed=1000, transcendentals=0)
PARAMS = pltpu.CompilerParams(vmem_limit_bytes=24 * 1024 * 1024)


def staged(kernel, shapes, operands, gate):
    arrays, picks = [pair[0] for pair in operands], [pair[1] for pair in operands]
    slots = [
        pltpu.VMEM(array.shape if pick is None else array.shape[1:], array.dtype)
        for array, pick in operands
    ]
    return pl.pallas_call(
        functools.partial(staged_kernel, kernel, picks, len(shapes)),
        out_shape=shapes,
        in_specs=[FAR] * (len(arrays) + 1),
        out_specs=[VMEM] * len(shapes),
        scratch_shapes=slots + [pltpu.SemaphoreType.DMA((len(picks),))],
        cost_estimate=LIGHT,
        compiler_params=PARAMS,
    )(*arrays, gate)


def on_core(kernel, shapes, operands, scratch=()):
    return pl.pallas_call(
        kernel,
        out_shape=shapes,
        in_specs=[VMEM] * len(operands),
        out_specs=[VMEM] * len(shapes),
        scratch_shapes=list(scratch),
        cost_estimate=LIGHT,
        compiler_params=PARAMS,
    )(*operands)


def choose(tick, plan, weights, gate):
    shapes = [jax.ShapeDtypeStruct(item.shape[-2:], item.dtype) for item in weights]
    shapes.append(jax.ShapeDtypeStruct((8, 128), jnp.float32))
    return pl.pallas_call(
        functools.partial(choose_kernel, tick),
        out_shape=shapes,
        in_specs=[pl.BlockSpec(memory_space=pltpu.SMEM)] + [FAR] * (len(weights) + 1),
        out_specs=[VMEM] * len(shapes),
        scratch_shapes=[pltpu.SemaphoreType.DMA((len(weights),))],
        cost_estimate=LIGHT,
        compiler_params=PARAMS,
    )(plan, *weights, gate)


def bf16(*shape):
    return jax.ShapeDtypeStruct(shape, jnp.bfloat16)


def f32(*shape):
    return jax.ShapeDtypeStruct(shape, jnp.float32)


def on_device(cot_in, saved_inputs, queries, keys, values, docs, plan, w_value, w_out, norm_gain):
    phases = lax.axis_size("section")
    members = lax.axis_size("tensor")
    chips = members // 2
    far = chips // 2
    rows, width = cot_in.shape
    length = rows * members
    half = length // 2
    heads = queries.shape[2] // HD
    hold = lax.optimization_barrier

    def swap(block):
        return lax.ppermute(block, "tensor", [(t, t ^ 1) for t in range(members)])

    def along(block, by):
        return lax.ppermute(block, "section", [(s, (s + by) % phases) for s in range(phases)])

    def hop(block, steps, back):
        pairs = []
        for section in range(phases):
            for z in range(chips):
                up, down = (z + steps) % chips, (z - steps) % chips if steps != far else z
                base = (section - back) % phases * members
                pairs.append((section * members + 2 * z, base + 2 * up))
                pairs.append((section * members + 2 * z + 1, base + 2 * down + 1))
        return lax.ppermute(block, ("section", "tensor"), pairs)

    def attention_ready(tick, gate):
        return staged(
            functools.partial(softmax_kernel, rows, chips),
            [f32(heads, length, length), bf16(heads, length, length)],
            [(item, tick) for item in (queries, keys, docs)],
            gate,
        )

    def grads(chance, grad_out, tick, gate):
        return staged(
            functools.partial(grads_kernel, rows, chips),
            [bf16(*queries.shape[1:]), bf16(*keys.shape[1:])],
            [(chance, None), (grad_out, None)]
            + [(item, tick) for item in (queries, keys, values)],
            gate,
        )

    def gather(pair, back, done):
        moved = [hop(pair, k, back) for k in range(far, 0, -1)]
        return hold((moved, done))

    def scatter(blocks, done):
        *near, edge = blocks
        relayed = lax.ppermute(
            edge, "tensor", [(2 * z, 2 * ((z + 1) % chips)) for z in range(chips)]
        )
        near[-1] = on_core(add_kernel, [bf16(2 * rows, width)], (near[-1], relayed))[0]
        moved = [hop(block, 1 + i, 0) for i, block in enumerate(near)]
        return hold((moved + [edge], done))

    other = swap(cot_in)
    other, *later = hold((other, w_value, w_out))
    away_value, away_out = (swap(item) for item in later)
    pair = on_core(order_kernel, [bf16(2 * rows, width)], (cot_in, other))[0]
    weights = [w_out, away_out, w_value, away_value]
    query_list = []
    key_list = []
    for tick in range(TICKS):
        last = tick == TICKS - 1
        if tick == 0:
            chosen = choose(0, plan, weights, pair)
            done = attention_ready(0, chosen[-1]), chosen
        elif tick == 1:
            done = attention_ready(2, pair)
        else:
            done = ()
        parts, done = gather(pair, 1 if tick else 0, done)
        if tick == 0:
            ready, chosen = done
        elif tick == 1:
            ready_last = done
        own_out, pair_out, own_value, pair_value, _ = chosen
        chance, low_t = ready
        keep, send = on_core(
            out_kernel,
            [bf16(half, heads * HD)] * 2,
            [*parts, own_out, pair_out],
            [pltpu.VMEM((half, width), jnp.bfloat16)],
        )
        grad_out, value_keep, value_send = on_core(
            value_kernel,
            [bf16(length, heads * HD), bf16(half, HD), bf16(half, HD)],
            (keep, swap(send), low_t),
        )
        if tick:
            odd = parts[0]
            value_away, even = hold((swap(value_send), swap(odd)))
        else:
            even = odd = pair
            value_away, inputs_away = hold((swap(value_send), swap(saved_inputs)))
        blocks = on_core(
            partial_kernel,
            [bf16(2 * rows, width)] * far,
            (value_keep, value_away, own_value, pair_value),
        )
        gate = blocks[-1]
        found = grads(chance, grad_out, tick, gate)
        lines = staged(
            lines_kernel,
            [bf16(2 * rows, width)],
            [(saved_inputs, tick), (inputs_away, tick)],
            gate,
        )[0]
        if last:
            done = jnp.stack(query_list + [found[0]]), jnp.stack(key_list + [found[1]])
        elif tick == 0:
            done = found, choose(1, plan, weights, gate), attention_ready(1, gate), inputs_away
        else:
            done = found, choose(2, plan, weights, gate)
        gain = choose(tick, plan, [norm_gain], gate)[0]
        done = done, lines, even, gain
        terms, (done, lines, even, gain) = scatter(blocks, done)
        total = on_core(sum_kernel, [bf16(2 * rows, width)], terms)[0]
        if last:
            query, key = done
        else:
            found, chosen = done[:2]
            if tick == 0:
                ready, inputs_away = done[2:]
            else:
                ready = ready_last
            query_list.append(found[0])
            key_list.append(found[1])
        pair, mine = on_core(
            norm_kernel,
            [bf16(2 * rows, width), bf16(rows, width)],
            (total, swap(total), lines, gain, even, odd),
        )
    return along(mine, -1), query, key


def solution(mesh):
    return jax.shard_map(
        on_device,
        mesh=mesh,
        in_specs=(
            P(("section", "tensor"), None),
            P(None, ("section", "tensor"), None),
            P(None, "section", "tensor"),
            P(None, "section", "tensor"),
            P(None, "section", "tensor"),
            P(None, "section", None),
            P(None, "section"),
            P(None, "section", None, "tensor"),
            P(None, "section", "tensor", None),
            P(None, "section", None),
        ),
        out_specs=(
            P(("section", "tensor"), None),
            P(None, "section", "tensor"),
            P(None, "section", "tensor"),
        ),
        check_vma=False,
    )
```

```python
import functools

import jax
import jax.numpy as jnp
from jax import lax
from jax.experimental import pallas as pl
from jax.experimental.pallas import tpu as pltpu
from jax.sharding import PartitionSpec as P

HD = 128
TICKS = 3
SCALE = 144.0 ** (-0.5)
EPS = 1e-06
NEGATIVE = -1e30
VMEM = pl.BlockSpec(memory_space=pltpu.VMEM)


def dot_t(a, b):
    return lax.dot_general(a, b, (((1,), (1,)), ((), ())), preferred_element_type=jnp.float32)


def dot_n(a, b):
    return lax.dot_general(a, b, (((1,), (0,)), ((), ())), preferred_element_type=jnp.float32)


def token_order(place, rank, rows, chips, direction):
    length = 2 * rows * chips
    half, size, far = length // 2, 2 * rows, chips // 2
    chip, own = rank // 2, rank % 2
    core = jnp.where(place < half, own, 1 - own)
    inner = jnp.where(place < half, place, place - half)
    part = inner // size
    within = inner - part * size
    near = (chip + direction * (1 - 2 * core) * (far - part) + chips) % chips
    edge = jnp.where(core == 0, (chip + far) % chips, chip)
    return jnp.where(part == 0, edge, near) * size + within


def softmax_kernel(rows, chips, wait, q_ref, k_ref, docs_ref, chance_ref, low_t_ref):
    length = q_ref.shape[0]
    rank = lax.axis_index("tensor")
    down = lax.broadcasted_iota(jnp.int32, (length, length), 0)
    across = lax.broadcasted_iota(jnp.int32, (length, length), 1)
    key_hot = (token_order(down, rank, rows, chips, 1) == across).astype(jnp.bfloat16)
    query_hot = (token_order(across, rank, rows, chips, -1) == down).astype(jnp.bfloat16)
    wait()
    line = docs_ref[...]
    column = jnp.sum(jnp.where(down == across, line, 0), axis=1, keepdims=True)
    allowed = (down >= across) & (column == line)
    for head in range(q_ref.shape[1] // HD):
        scores = dot_t(q_ref[:, head * HD : (head + 1) * HD], k_ref[...]) * SCALE
        scores = jnp.where(allowed, scores, NEGATIVE)
        expsum = jnp.exp(scores - jnp.max(scores, axis=-1, keepdims=True))
        chance = expsum / jnp.sum(expsum, axis=-1, keepdims=True)
        chance_ref[head] = chance
        turned = dot_t(key_hot, chance.astype(jnp.bfloat16)).astype(jnp.bfloat16)
        low_t_ref[head] = dot_n(turned, query_hot).astype(jnp.bfloat16)


def grads_kernel(rows, chips, wait, chance_ref, go_ref, q_ref, k_ref, v_ref, gq_ref, gk_ref):
    length = q_ref.shape[0]
    rank = lax.axis_index("tensor")
    down = lax.broadcasted_iota(jnp.int32, (length, length), 0)
    across = lax.broadcasted_iota(jnp.int32, (length, length), 1)
    query_hot = (token_order(across, rank, rows, chips, -1) == down).astype(jnp.bfloat16)
    wait()
    grad_out = dot_n(query_hot, go_ref[...]).astype(jnp.bfloat16)
    total = jnp.zeros(gk_ref.shape, jnp.float32)
    for head in range(q_ref.shape[1] // HD):
        columns = slice(head * HD, (head + 1) * HD)
        chance = chance_ref[head]
        grad = grad_out[:, columns]
        attended = dot_n(chance.astype(jnp.bfloat16), v_ref[...])
        row_dot = jnp.sum(grad.astype(jnp.float32) * attended, axis=-1, keepdims=True)
        grad_chance = dot_t(grad, v_ref[...])
        grad_scores = (chance * (grad_chance - row_dot)).astype(jnp.bfloat16)
        gq_ref[:, columns] = (dot_n(grad_scores, k_ref[...]) * SCALE).astype(jnp.bfloat16)
        total = total + lax.dot_general(
            grad_scores,
            q_ref[:, columns],
            (((0,), (0,)), ((), ())),
            preferred_element_type=jnp.float32,
        )
    gk_ref[...] = (total * SCALE).astype(jnp.bfloat16)


def order_kernel(a_ref, b_ref, pair_ref):
    rows = a_ref.shape[0]
    first = lax.axis_index("tensor") % 2 == 0
    pair_ref[:rows] = jnp.where(first, a_ref[...], b_ref[...])
    pair_ref[rows:] = jnp.where(first, b_ref[...], a_ref[...])


def out_kernel(count, *refs):
    *refs, mine_ref = refs
    parts, rest = refs[:count], refs[count:]
    size = parts[0].shape[0]
    for i, part in enumerate(parts):
        mine_ref[i * size : (i + 1) * size] = part[...]
    products = len(rest) // 2
    for weight, out in zip(rest[:products], rest[products:]):
        out[...] = dot_t(mine_ref[...], weight[...]).astype(jnp.bfloat16)


def value_kernel(keep_ref, recv_ref, low_t_ref, go_ref, own_ref, away_ref):
    half = keep_ref.shape[0]
    go_ref[:half] = keep_ref[...]
    go_ref[half:] = recv_ref[...]
    total = jnp.zeros((2 * half, HD), jnp.float32)
    for head in range(low_t_ref.shape[0]):
        total = total + dot_n(low_t_ref[head], go_ref[:, head * HD : (head + 1) * HD])
    total = total.astype(jnp.bfloat16)
    own_ref[...] = total[:half]
    away_ref[...] = total[half:]


def partial_kernel(gv_ref, gv_pair_ref, own_ref, pair_ref, *outs):
    total = dot_t(gv_ref[...], own_ref[...]) + dot_t(gv_pair_ref[...], pair_ref[...])
    total = total.astype(jnp.bfloat16)
    size = outs[0].shape[0]
    for i, out in enumerate(outs):
        at = (len(outs) - 1 - i) * size
        out[...] = total[at : at + size]


def add_kernel(own_ref, relayed_ref, total_ref):
    first = lax.axis_index("tensor") % 2 == 0
    own = own_ref[...].astype(jnp.float32)
    relayed = relayed_ref[...].astype(jnp.float32)
    total_ref[...] = (own + jnp.where(first, relayed, 0.0)).astype(jnp.bfloat16)


def sum_kernel(*refs):
    *near, edge_ref, total_ref = refs
    first = lax.axis_index("tensor") % 2 == 0
    total = jnp.where(first, 0.0, edge_ref[...].astype(jnp.float32))
    for ref in near:
        total = total + ref[...].astype(jnp.float32)
    total_ref[...] = total.astype(total_ref.dtype)


def lines_kernel(wait, own_ref, other_ref, pair_ref):
    wait()
    order_kernel(own_ref, other_ref, pair_ref)


def norm_kernel(a_ref, b_ref, x_ref, gain_ref, even_ref, odd_ref, new_ref, mine_ref):
    rows = mine_ref.shape[0]
    first = lax.axis_index("tensor") % 2 == 0
    inputs = x_ref[...].astype(jnp.float32)
    inverse = lax.rsqrt(jnp.mean(inputs * inputs, -1, keepdims=True) + EPS)
    scaled = a_ref[...].astype(jnp.float32) + b_ref[...].astype(jnp.float32)
    scaled = scaled * gain_ref[...].astype(jnp.float32)
    inner = jnp.mean(scaled * inputs, -1, keepdims=True)
    current = jnp.where(first, even_ref[...], odd_ref[...]).astype(jnp.float32)
    updated = (
        current + inverse * scaled - inputs * (inverse * inverse * inverse * inner)
    ).astype(jnp.bfloat16)
    new_ref[...] = updated
    mine_ref[...] = jnp.where(first, updated[:rows], updated[rows:])


def staged_kernel(kernel, picks, count, *refs):
    sources = refs[: len(picks)]
    outs = refs[-count - len(picks) - 1 : -len(picks) - 1]
    held, sems = refs[-len(picks) - 1 : -1], refs[-1]
    copies = [
        pltpu.make_async_copy(source if pick is None else source.at[pick], slot, sems.at[i])
        for i, (pick, source, slot) in enumerate(zip(picks, sources, held))
    ]
    for copy in copies:
        copy.start()

    def wait():
        for copy in copies:
            copy.wait()

    kernel(wait, *held, *outs)


def choose_kernel(tick, plan_ref, *refs):
    chosen = plan_ref[tick, 0]
    count = (len(refs) - 3) // 2
    sources, outs, mark, sems = refs[:count], refs[count + 1 : -2], refs[-2], refs[-1]
    mark[...] = jnp.zeros_like(mark)
    copies = []
    for i, (source, out) in enumerate(zip(sources, outs)):
        view = source.at[chosen, 0] if len(source.shape) == 4 else source.at[chosen]
        copies.append(pltpu.make_async_copy(view, out, sems.at[i]))
    for copy in copies:
        copy.start()
    for copy in copies:
        copy.wait()


FAR = pl.BlockSpec(memory_space=pltpu.HBM)
LIGHT = pl.CostEstimate(flops=1000, bytes_accessed=1000, transcendentals=0)
PARAMS = pltpu.CompilerParams(vmem_limit_bytes=24 * 1024 * 1024)
WIDE = pltpu.CompilerParams(vmem_limit_bytes=56 * 1024 * 1024)


def staged(kernel, shapes, operands, gate):
    arrays, picks = [pair[0] for pair in operands], [pair[1] for pair in operands]
    slots = [
        pltpu.VMEM(array.shape if pick is None else array.shape[1:], array.dtype)
        for array, pick in operands
    ]
    return pl.pallas_call(
        functools.partial(staged_kernel, kernel, picks, len(shapes)),
        out_shape=shapes,
        in_specs=[FAR] * (len(arrays) + 1),
        out_specs=[VMEM] * len(shapes),
        scratch_shapes=slots + [pltpu.SemaphoreType.DMA((len(picks),))],
        cost_estimate=LIGHT,
        compiler_params=PARAMS,
    )(*arrays, gate)


def on_core(kernel, shapes, operands, scratch=(), params=PARAMS):
    return pl.pallas_call(
        kernel,
        out_shape=shapes,
        in_specs=[VMEM] * len(operands),
        out_specs=[VMEM] * len(shapes),
        scratch_shapes=list(scratch),
        cost_estimate=LIGHT,
        compiler_params=params,
    )(*operands)


def choose(tick, plan, weights, gate):
    shapes = [jax.ShapeDtypeStruct(item.shape[-2:], item.dtype) for item in weights]
    shapes.append(jax.ShapeDtypeStruct((8, 128), jnp.float32))
    return pl.pallas_call(
        functools.partial(choose_kernel, tick),
        out_shape=shapes,
        in_specs=[pl.BlockSpec(memory_space=pltpu.SMEM)] + [FAR] * (len(weights) + 1),
        out_specs=[VMEM] * len(shapes),
        scratch_shapes=[pltpu.SemaphoreType.DMA((len(weights),))],
        cost_estimate=LIGHT,
        compiler_params=PARAMS,
    )(plan, *weights, gate)


def bf16(*shape):
    return jax.ShapeDtypeStruct(shape, jnp.bfloat16)


def f32(*shape):
    return jax.ShapeDtypeStruct(shape, jnp.float32)


def on_device(cot_in, saved_inputs, queries, keys, values, docs, plan, w_value, w_out, norm_gain):
    phases = lax.axis_size("section")
    members = lax.axis_size("tensor")
    chips = members // 2
    far = chips // 2
    rows, width = cot_in.shape
    length = rows * members
    half = length // 2
    heads = queries.shape[2] // HD
    hold = lax.optimization_barrier

    def swap(block):
        return lax.ppermute(block, "tensor", [(t, t ^ 1) for t in range(members)])

    def along(block, by):
        return lax.ppermute(block, "section", [(s, (s + by) % phases) for s in range(phases)])

    def hop(block, steps, back):
        pairs = []
        for section in range(phases):
            for z in range(chips):
                up, down = (z + steps) % chips, (z - steps) % chips if steps != far else z
                base = (section - back) % phases * members
                pairs.append((section * members + 2 * z, base + 2 * up))
                pairs.append((section * members + 2 * z + 1, base + 2 * down + 1))
        return lax.ppermute(block, ("section", "tensor"), pairs)

    def attention_ready(tick, gate):
        return staged(
            functools.partial(softmax_kernel, rows, chips),
            [f32(heads, length, length), bf16(heads, length, length)],
            [(item, tick) for item in (queries, keys, docs)],
            gate,
        )

    def grads(chance, grad_out, tick, gate):
        return staged(
            functools.partial(grads_kernel, rows, chips),
            [bf16(*queries.shape[1:]), bf16(*keys.shape[1:])],
            [(chance, None), (grad_out, None)]
            + [(item, tick) for item in (queries, keys, values)],
            gate,
        )

    def gather(pair, back, done):
        moved = [hop(pair, k, back) for k in range(far, 0, -1)]
        return hold((moved, done))

    def scatter(blocks, done):
        *near, edge = blocks
        moved = [hop(block, 1 + i, 0) for i, block in enumerate(near)]
        return hold((moved + [edge], done))

    other = swap(cot_in)
    other, *later = hold((other, w_value, w_out))
    away_value, away_out = (swap(item) for item in later)
    pair = on_core(order_kernel, [bf16(2 * rows, width)], (cot_in, other), params=WIDE)[0]
    weights = [w_out, away_out, w_value, away_value]
    query_list = []
    key_list = []
    for tick in range(TICKS):
        last = tick == TICKS - 1
        if tick == 0:
            chosen = choose(0, plan, weights, pair)
            done = attention_ready(0, chosen[-1]), chosen
        elif tick == 1:
            done = attention_ready(2, pair)
        else:
            done = ()
        parts, done = gather(pair, 1 if tick else 0, done)
        if tick == 0:
            ready, chosen = done
        elif tick == 1:
            ready_last = done
        own_out, pair_out, own_value, pair_value, _ = chosen
        chance, low_t = ready
        groups = [[pair_out], [own_out]] if tick else [[pair_out, own_out]]
        send, keep = [
            product
            for group in groups
            for product in on_core(
                functools.partial(out_kernel, len(parts)),
                [bf16(half, heads * HD)] * len(group),
                [*parts, *group],
                [pltpu.VMEM((half, width), jnp.bfloat16)],
            )
        ]
        grad_out, value_keep, value_send = on_core(
            value_kernel,
            [bf16(length, heads * HD), bf16(half, HD), bf16(half, HD)],
            (keep, swap(send), low_t),
        )
        if tick:
            odd, value_send = hold((parts[0], value_send))
            value_away, even = hold((swap(value_send), swap(odd)))
        else:
            even = odd = pair
            value_away, inputs_away = hold((swap(value_send), swap(saved_inputs)))
        blocks = on_core(
            partial_kernel,
            [bf16(2 * rows, width)] * far,
            (value_keep, value_away, own_value, pair_value),
        )
        *near, edge = blocks
        relayed = lax.ppermute(
            edge, "tensor", [(2 * z, 2 * ((z + 1) % chips)) for z in range(chips)]
        )
        near[-1] = on_core(add_kernel, [bf16(2 * rows, width)], (near[-1], relayed))[0]
        gate = near[-1]
        found = grads(chance, grad_out, tick, gate)
        lines = staged(
            lines_kernel,
            [bf16(2 * rows, width)],
            [(saved_inputs, tick), (inputs_away, tick)],
            gate,
        )[0]
        if last:
            done = jnp.stack(query_list + [found[0]]), jnp.stack(key_list + [found[1]])
        elif tick == 0:
            done = found, choose(1, plan, weights, gate), attention_ready(1, gate), inputs_away
        else:
            done = found, choose(2, plan, weights, gate)
        gain = choose(tick, plan, [norm_gain], gate)[0]
        done = done, lines, even, gain
        terms, (done, lines, even, gain) = scatter([*near, edge], done)
        total = on_core(sum_kernel, [bf16(2 * rows, width)], terms)[0]
        if last:
            query, key = done
        else:
            found, chosen = done[:2]
            if tick == 0:
                ready, inputs_away = done[2:]
            else:
                ready = ready_last
            query_list.append(found[0])
            key_list.append(found[1])
        pair, mine = on_core(
            norm_kernel,
            [bf16(2 * rows, width), bf16(rows, width)],
            (total, swap(total), lines, gain, even, odd),
        )
    return along(mine, -1), query, key


def solution(mesh):
    return jax.shard_map(
        on_device,
        mesh=mesh,
        in_specs=(
            P(("section", "tensor"), None),
            P(None, ("section", "tensor"), None),
            P(None, "section", "tensor"),
            P(None, "section", "tensor"),
            P(None, "section", "tensor"),
            P(None, "section", None),
            P(None, "section"),
            P(None, "section", None, "tensor"),
            P(None, "section", "tensor", None),
            P(None, "section", None),
        ),
        out_specs=(
            P(("section", "tensor"), None),
            P(None, "section", "tensor"),
            P(None, "section", "tensor"),
        ),
        check_vma=False,
    )
```
